512 devices in a mesh: row: 32 (over x_lo, z), col: 16 (over x_hi, y, core).
Axes of the slice: x: 4 (x_hi: 2, x_lo: 2; x = x_hi * 2 + x_lo), y: 4, z: 16, core: 2. Of those that a mesh axis runs over, the one named last changes fastest.
Arguments:
- features: bfloat16 [65536, 128], P(('col', 'row')), may hold values from -6 to 6
- grad_out: bfloat16 [65536, 256], P(('row', 'col')), may hold values from -6 to 6
- row_scale: float32 [65536], P(('row', 'col')), may hold values from 0.00390625 to 0.0390625
- out_bias: float32 [256], replicated, may hold values from -3 to 3
- weight: bfloat16 [128, 256], replicated, may hold values from -0.5 to 0.5
- tile_vals: bfloat16 [32, 16, 128, 128, 128], P('row', 'col'), as said below
- tile_rows: int32 [32, 16, 128], P('row', 'col'), may hold values from 0 to 15, as said below
- tile_cols: int32 [32, 16, 128], P('row', 'col'), may hold values from 0 to 31, as said below
- tile_count: int32 [32, 16], P('row', 'col'), may hold values from 16 to 128, as said below
Outputs:
- output: bfloat16 [65536, 256], P(('row', 'col'))
- grad_features: bfloat16 [65536, 128], P(('col', 'row'))
- grad_weight: float32 [128, 256], replicated
The draws below stay inside these ranges and needn't reach their ends.
Inputs may be any that keep to these rules, and one draw needn't show every extreme that they name: `tile_count`: every device holds from 128 // 8 (at least 1) to 128 tiles, and some device holds exactly 128; slots at and beyond a device's count hold no tile. The pairs (tile_rows, tile_cols) of one device's slots are all different. `tile_cols`: see tile_rows. `tile_vals`: about half of a tile's entries are zero.
All inputs are finite; a program needn't handle non-finite values.
Results may differ from the reference program's by a relative error of at most 0.029.
Values may be sent and summed in bfloat16 or wider, within the bound.
No kernel may reach another device: no remote copies, remote signals or barrier semaphores. Data moves between devices by JAX's collectives and lax.ppermute only.
A program may use at most 64 MiB of HBM per device.

```python
import math
import jax
import jax.numpy as jnp
from jax import lax

D_IN = 128
D_OUT = 256
BLK = 128
NODES = 65536
ROW_BLOCKS = 16
COL_BLOCKS = 32
TILE_SLOTS = 128
N_ROW = 32
N_COL = 16


def tile_slots(key):
    base = jax.random.fold_in(key, 7)
    keys = jax.random.split(base, N_ROW * N_COL)

    def choose(one_key):
        return jax.random.permutation(one_key, ROW_BLOCKS * COL_BLOCKS)[:TILE_SLOTS]
    orders = jax.vmap(choose)(keys)
    return orders.reshape(N_ROW, N_COL, TILE_SLOTS).astype(jnp.int32)


def draw_tile_rows(key, part):
    return (tile_slots(key) // COL_BLOCKS).astype(jnp.int32)


def draw_tile_cols(key, part):
    return (tile_slots(key) % COL_BLOCKS).astype(jnp.int32)


def draw_tile_count(key, part):
    first_key = jax.random.fold_in(key, 11)
    second_key = jax.random.fold_in(key, 13)
    third_key = jax.random.fold_in(key, 17)
    lowest = max(1, TILE_SLOTS // 8)
    base = jax.random.randint(first_key, (N_ROW * N_COL,), lowest, TILE_SLOTS // 2 + 1)
    heavy = jax.random.randint(second_key, (N_ROW * N_COL,), 0, 8) == 0
    forced = jax.random.randint(third_key, (), 0, N_ROW * N_COL)
    heavy = heavy | (jnp.arange(N_ROW * N_COL, dtype=jnp.int32) == forced)
    counts = jnp.where(heavy, TILE_SLOTS, base)
    return counts.reshape(N_ROW, N_COL).astype(jnp.int32)


def draw_tile_vals(key, part):
    shape = (N_ROW, N_COL, TILE_SLOTS, BLK, BLK)
    mask_key = jax.random.fold_in(key, 19)
    value_key = jax.random.fold_in(key, 23)
    present = jax.random.randint(mask_key, shape, 0, 2).astype(jnp.float32)
    values = jax.random.uniform(value_key, shape, jnp.float32, 0.5, 1.5)
    return (present * values).astype(jnp.bfloat16)


def block_scale(rng, extent, cuts, smallest, top_value):
    def one(axis_at, shards_of):
        heights = jax.random.uniform(jax.random.fold_in(jax.random.fold_in(rng, 6), axis_at), (shards_of,), jnp.float32, smallest / len(cuts), top_value / len(cuts))
        return jnp.repeat(jnp.exp(heights), extent[axis_at] // shards_of).reshape((-1,) + (1,) * (len(extent) - axis_at - 1))

    level = one(*cuts[0])
    for cut in cuts[1:]:
        level = level * one(*cut)
    return level


def gaussian(rng, dims, deviation, reach, cuts=(), kind=jnp.bfloat16):
    array = jax.random.normal(rng, dims, jnp.float32) * deviation
    if len(cuts) > 0:
        array = block_scale(rng, dims, cuts, -0.22, 0.18) * array
    return jnp.clip(array, min=-reach, max=reach).astype(kind)


def setup_inputs(seed: int = 0) -> dict:
    seeds = jax.random.split(jax.random.key(seed), 10)
    return {
        "features": gaussian(seeds[0], (NODES, D_IN), 1.0, 6.0, ((0, 512),)),
        "grad_out": gaussian(seeds[1], (NODES, D_OUT), 1.0, 6.0, ((0, 512),)),
        "row_scale": jnp.clip(jnp.exp(math.log(0.0390625) - 2.3025851 * jax.random.uniform(seeds[2], (NODES,), jnp.float32) ** block_scale(seeds[2], (NODES,), ((0, 512),), -0.2, 0.2)), 0.00390625, 0.0390625),
        "out_bias": gaussian(seeds[3], (D_OUT,), 0.5, 3.0, (), jnp.float32),
        "weight": gaussian(seeds[4], (D_IN, D_OUT), D_IN ** -0.5, 0.5),
        "tile_vals": draw_tile_vals(jax.random.fold_in(seeds[9], 71), 0),
        "tile_rows": draw_tile_rows(jax.random.fold_in(seeds[9], 71), 0),
        "tile_cols": draw_tile_cols(jax.random.fold_in(seeds[9], 71), 0),
        "tile_count": draw_tile_count(jax.random.fold_in(seeds[9], 71), 0),
    }


def reference(features, grad_out, row_scale, out_bias, weight, tile_vals, tile_rows, tile_cols, tile_count):
    transformed = jnp.dot(features, weight, preferred_element_type=jnp.float32).astype(jnp.bfloat16)
    flat_vals = tile_vals.reshape(N_ROW * N_COL, TILE_SLOTS, BLK, BLK)
    flat_rows = tile_rows.reshape(N_ROW * N_COL, TILE_SLOTS)
    flat_cols = tile_cols.reshape(N_ROW * N_COL, TILE_SLOTS)
    flat_count = tile_count.reshape(N_ROW * N_COL)
    device_ids = jnp.arange(N_ROW * N_COL, dtype=jnp.int32)
    slot_ids = jnp.arange(TILE_SLOTS, dtype=jnp.int32)
    row_ids = jnp.arange(ROW_BLOCKS, dtype=jnp.int32)
    col_ids = jnp.arange(COL_BLOCKS, dtype=jnp.int32)

    def forward_step(summed, inputs):
        values, rows_idx, cols_idx, total, device = inputs
        row_dev = (device // N_COL).astype(jnp.int32)
        col_dev = (device % N_COL).astype(jnp.int32)
        sources = lax.dynamic_slice_in_dim(transformed, col_dev * (COL_BLOCKS * BLK), COL_BLOCKS * BLK, 0)
        picked = sources.reshape(COL_BLOCKS, BLK, D_OUT)[cols_idx]
        product = jnp.einsum("tab,tbw->taw", values.astype(jnp.float32), picked.astype(jnp.float32), precision=lax.Precision.HIGHEST)
        active = slot_ids < total
        placing = ((rows_idx[None, :] == row_ids[:, None]) & active[None, :]).astype(jnp.float32)
        block = jnp.einsum("rt,taw->raw", placing, product, precision=lax.Precision.HIGHEST).reshape(ROW_BLOCKS * BLK, D_OUT)
        first = row_dev * (ROW_BLOCKS * BLK)
        current = lax.dynamic_slice_in_dim(summed, first, ROW_BLOCKS * BLK, 0)
        return lax.dynamic_update_slice_in_dim(summed, current + block, first, 0), None

    summed = lax.scan(forward_step, jnp.zeros((NODES, D_OUT), jnp.float32), (flat_vals, flat_rows, flat_cols, flat_count, device_ids))[0]
    hidden = row_scale[:, None] * summed + out_bias[None, :]
    sigma = jax.nn.sigmoid(hidden)
    output = (hidden * sigma).astype(jnp.bfloat16)
    d_hidden = grad_out.astype(jnp.float32) * sigma * (1.0 + hidden * (1.0 - sigma))
    scaled = (row_scale[:, None] * d_hidden).astype(jnp.bfloat16)

    def backward_step(col_total, inputs):
        values, rows_idx, cols_idx, total, device = inputs
        row_dev = (device // N_COL).astype(jnp.int32)
        col_dev = (device % N_COL).astype(jnp.int32)
        sources = lax.dynamic_slice_in_dim(scaled, row_dev * (ROW_BLOCKS * BLK), ROW_BLOCKS * BLK, 0)
        picked = sources.reshape(ROW_BLOCKS, BLK, D_OUT)[rows_idx]
        product = jnp.einsum("tab,taw->tbw", values.astype(jnp.float32), picked.astype(jnp.float32), precision=lax.Precision.HIGHEST)
        active = slot_ids < total
        placing = ((cols_idx[None, :] == col_ids[:, None]) & active[None, :]).astype(jnp.float32)
        block = jnp.einsum("ct,taw->caw", placing, product, precision=lax.Precision.HIGHEST).reshape(COL_BLOCKS * BLK, D_OUT)
        block = lax.optimization_barrier(block.astype(jnp.bfloat16)).astype(jnp.float32)
        first = col_dev * (COL_BLOCKS * BLK)
        current = lax.dynamic_slice_in_dim(col_total, first, COL_BLOCKS * BLK, 0)
        return lax.dynamic_update_slice_in_dim(col_total, current + block, first, 0), None

    col_total = lax.scan(backward_step, jnp.zeros((NODES, D_OUT), jnp.float32), (flat_vals, flat_rows, flat_cols, flat_count, device_ids))[0]
    rounded = col_total.astype(jnp.bfloat16)
    grad_features = jnp.dot(rounded, weight.T, preferred_element_type=jnp.float32).astype(jnp.bfloat16)
    grad_weight = jnp.dot(features.T, rounded, preferred_element_type=jnp.float32)
    return output, grad_features, grad_weight
```

```python
import jax
import jax.numpy as jnp
from jax import lax
from jax.experimental import pallas as pl
from jax.experimental.pallas import tpu as pltpu
from jax.sharding import Mesh
from jax.sharding import PartitionSpec as P

F32 = jnp.float32
BF16 = jnp.bfloat16
Z = ("zh", "zl")
ROW = ("xl",) + Z
COL = ("xh", "y", "core")
AXES = ROW + COL
SIZES = (2, 4, 4, 2, 4, 2)

E = 128
WIDE = 256
SLOTS = 128
GROUP = 16
CHUNKS = SLOTS // GROUP
NZ, NX, NC = 16, 2, 16
NR = NX * NZ
GW = 32
PACK = E + GW

ANY = pl.BlockSpec(memory_space=pl.ANY)
VMEM = pl.BlockSpec(memory_space=pltpu.VMEM)
SMEM = pl.BlockSpec(memory_space=pltpu.SMEM)
PARAMS = pltpu.CompilerParams(vmem_limit_bytes=40 * 1024 * 1024)


def split(x):
    high = x.astype(BF16)
    return high, (x - high.astype(F32)).astype(BF16)


def pack_weight_grad(piece):
    flat = jnp.concatenate([piece[:, :E], piece[:, E:]], axis=0)
    high, low = split(flat)
    return jnp.concatenate([high, low], axis=0)


def unpack_weight_grad(packed):
    wide = packed.astype(F32)
    return wide[:16] + wide[16:]


def sweep(count, chunk_copies, tile_product, add):
    def chunk_step(c, carry):
        chunk_copies(c).wait()
        left = count - c * GROUP

        @pl.when(left >= GROUP)
        def _():
            for u0 in range(0, GROUP, 4):
                products = [tile_product(c, u, c * GROUP + u) for u in range(u0, u0 + 4)]
                for k, product in enumerate(products):
                    add(c * GROUP + u0 + k, product)

        @pl.when(left < GROUP)
        def _():
            def one(u, inner):
                add(c * GROUP + u, tile_product(c, u, c * GROUP + u))
                return inner

            lax.fori_loop(0, left, one, 0)

        return carry

    lax.fori_loop(0, CHUNKS, chunk_step, 0)


def forward_kernel(count, rows, cols, own, tiles, mine, peer, out, held, source, total, tile_sem, source_sem):
    def tile_copy(c):
        return pltpu.make_async_copy(tiles.at[c], held.at[c], tile_sem.at[c])

    near = pltpu.make_async_copy(mine, source.at[pl.ds(0, NZ)], source_sem.at[0])
    far = pltpu.make_async_copy(peer, source.at[pl.ds(NZ, NZ)], source_sem.at[1])
    near.start()
    far.start()
    for c in range(CHUNKS):
        tile_copy(c).start()
    total[...] = jnp.zeros_like(total)
    flip = own[0] * NZ
    near.wait()
    far.wait()

    def product(c, u, t):
        place = jnp.bitwise_xor(cols[t], flip)
        return jnp.dot(held[c, u], source[place], preferred_element_type=F32)

    def add(t, value):
        total[rows[t]] += value

    sweep(count[0], tile_copy, product, add)
    out[...] = total[...].astype(BF16)


def node_kernel(terms, scale, bias, weight, grad_out, output, pack):
    gathered = terms[0].astype(F32)
    for k in range(1, NC):
        gathered = gathered + terms[k].astype(F32)
    high, low = split(gathered)
    w = weight[...]
    summed = jnp.dot(high, w, preferred_element_type=F32) + jnp.dot(low, w, preferred_element_type=F32)
    r = scale[...]
    hidden = r * summed + bias[...]
    s = jax.nn.sigmoid(hidden)
    output[...] = (hidden * s).astype(BF16)
    d_hidden = grad_out[...].astype(F32) * s * (1.0 + hidden * (1.0 - s))
    scaled = (r * d_hidden).astype(BF16)
    back = lax.dot_general(w, scaled, (((1,), (1,)), ((), ())), preferred_element_type=F32).astype(BF16)
    first = (((0,), (0,)), ((), ()))
    grad = lax.dot_general(high, scaled, first, preferred_element_type=F32)
    grad = grad + lax.dot_general(low, scaled, first, preferred_element_type=F32)
    for k in range(NC):
        pack[k, pl.ds(0, E)] = back
        pack[k, pl.ds(E, GW)] = pack_weight_grad(grad[8 * k : 8 * k + 8])


def backward_kernel(count, rows, cols, own, tiles, packed, keep, send, held, source, total, tile_sem, source_sem):
    def tile_copy(c):
        return pltpu.make_async_copy(tiles.at[c], held.at[c], tile_sem.at[c])

    arrive = pltpu.make_async_copy(packed, source, source_sem.at[0])
    arrive.start()
    for c in range(CHUNKS):
        tile_copy(c).start()
    total[...] = jnp.zeros_like(total)
    flip = own[0] * NZ
    arrive.wait()

    def product(c, u, t):
        return jnp.dot(source[rows[t], pl.ds(0, E)], held[c, u], preferred_element_type=F32)

    def add(t, value):
        total[jnp.bitwise_xor(cols[t], flip)] += value

    sweep(count[0], tile_copy, product, add)
    grad = unpack_weight_grad(source[0, pl.ds(E, GW)])
    for k in range(1, NC):
        grad = grad + unpack_weight_grad(source[k, pl.ds(E, GW)])
    high, low = split(grad)
    for z in range(NZ):
        keep[pl.ds(z * E, E)] = total[z].astype(BF16)
        send[pl.ds(z * E, E)] = total[NZ + z].astype(BF16)
    for ref in (keep, send):
        ref[pl.ds(NZ * E, 16)] = high
        ref[pl.ds(NZ * E + 16, 16)] = low


def pair_kernel(keep, came, pack):
    for z in range(NZ):
        rows = pl.ds(z * E, E)
        pack[z, pl.ds(0, E)] = (keep[rows].astype(F32) + came[rows].astype(F32)).astype(BF16)
    tail = pl.ds(NZ * E, GW)
    high, low = split(unpack_weight_grad(keep[tail]) + unpack_weight_grad(came[tail]))
    for z in range(NZ):
        pack[z, pl.ds(E, 16)] = high
        pack[z, pl.ds(E + 16, 16)] = low


def last_kernel(terms, grad_features, grad_piece):
    value = terms[0].astype(F32)
    for z in range(1, NZ):
        value = value + terms[z].astype(F32)
    grad_features[...] = value[:E].T.astype(BF16)
    both = value[E : E + 16] + value[E + 16 : E + 32]
    piece = jnp.concatenate([both[:8], both[8:]], axis=1)
    for k in range(NC):
        grad_piece[k] = piece


def shape(dims, kind=BF16):
    return jax.ShapeDtypeStruct(dims, kind)


def on_device(features, grad_out, row_scale, out_bias, weight, tile_vals, tile_rows, tile_cols, tile_count):
    tiles = tile_vals.reshape(CHUNKS, GROUP, E, E)
    rows = tile_rows.reshape(SLOTS)
    cols = tile_cols.reshape(SLOTS)
    count = tile_count.reshape(1)
    own = lax.axis_index("xl").astype(jnp.int32).reshape(1)
    swap = [(0, 1), (1, 0)]

    copies = jnp.broadcast_to(features[None], (NZ, E, E))
    mine = lax.all_to_all(copies, Z, 0, 0, tiled=True)
    peer = lax.ppermute(mine, "xl", swap)
    sems = [pltpu.SemaphoreType.DMA((CHUNKS,)), pltpu.SemaphoreType.DMA((2,))]
    partial = pl.pallas_call(
        forward_kernel,
        out_shape=shape((NC, E, E)),
        in_specs=[SMEM] * 4 + [ANY] * 3,
        out_specs=VMEM,
        scratch_shapes=[
            pltpu.VMEM((CHUNKS, GROUP, E, E), BF16),
            pltpu.VMEM((NR, E, E), BF16),
            pltpu.VMEM((NC, E, E), F32),
        ]
        + sems,
        compiler_params=PARAMS,
        name="forward_sweep",
    )(count, rows, cols, own, tiles, mine, peer)
    terms = lax.all_to_all(partial, COL, 0, 0, tiled=True)
    output, pack = pl.pallas_call(
        node_kernel,
        out_shape=(shape((E, WIDE)), shape((NC, PACK, E))),
        in_specs=[VMEM] * 5,
        out_specs=(VMEM, VMEM),
        compiler_params=PARAMS,
        name="node_update",
    )(terms, row_scale.reshape(E, 1), out_bias.reshape(1, WIDE), weight, grad_out)
    packed = lax.all_to_all(pack, COL, 0, 0, tiled=True)
    line = shape((NZ * E + GW, E))
    keep, send = pl.pallas_call(
        backward_kernel,
        out_shape=(line, line),
        in_specs=[SMEM] * 4 + [ANY] * 2,
        out_specs=(VMEM, VMEM),
        scratch_shapes=[
            pltpu.VMEM((CHUNKS, GROUP, E, E), BF16),
            pltpu.VMEM((NC, PACK, E), BF16),
            pltpu.VMEM((NR, E, E), F32),
        ]
        + sems,
        compiler_params=PARAMS,
        name="backward_sweep",
    )(count, rows, cols, own, tiles, packed)
    came = lax.ppermute(send, "xl", swap)
    pairs = pl.pallas_call(
        pair_kernel,
        out_shape=shape((NZ, PACK, E)),
        in_specs=[VMEM] * 2,
        out_specs=VMEM,
        compiler_params=PARAMS,
        name="pair_sum",
    )(keep, came)
    last = lax.all_to_all(pairs, Z, 0, 0, tiled=True)
    grad_features, piece = pl.pallas_call(
        last_kernel,
        out_shape=(shape((E, E)), shape((NC, 8, WIDE), F32)),
        in_specs=[VMEM],
        out_specs=(VMEM, VMEM),
        compiler_params=PARAMS,
        name="last_sum",
    )(last)
    grad_weight = lax.all_to_all(piece, COL, 0, 0, tiled=True).reshape(E, WIDE)
    return output, grad_features, grad_weight


def solution(mesh):
    fine = Mesh(mesh.devices.reshape(SIZES), AXES)
    by_row = ROW + COL
    by_col = COL + ROW
    return jax.shard_map(
        on_device,
        mesh=fine,
        in_specs=(
            P(by_col, None),
            P(by_row, None),
            P(by_row),
            P(),
            P(),
            P(ROW, COL, None, None, None),
            P(ROW, COL, None),
            P(ROW, COL, None),
            P(ROW, COL),
        ),
        out_specs=(P(by_row, None), P(by_col, None), P()),
        check_vma=False,
    )
```

```python
import jax
import jax.numpy as jnp
from jax import lax
from jax.experimental import pallas as pl
from jax.experimental.pallas import tpu as pltpu
from jax.sharding import Mesh
from jax.sharding import PartitionSpec as P

F32 = jnp.float32
BF16 = jnp.bfloat16
Z = ("zh", "zl")
ROW = ("xl",) + Z
CHIP = ("xh", "y")
COL = CHIP + ("core",)
AXES = ROW + COL
SIZES = (2, 4, 4, 2, 4, 2)

E = 128
WIDE = 256
SLOTS = 128
GROUP = 16
CHUNKS = SLOTS // GROUP
NZ, NX, NC = 16, 2, 16
NR = NX * NZ
GW = 32
PACK = E + 2 * GW
NCHIP = 8

ANY = pl.BlockSpec(memory_space=pl.ANY)
VMEM = pl.BlockSpec(memory_space=pltpu.VMEM)
SMEM = pl.BlockSpec(memory_space=pltpu.SMEM)
PARAMS = pltpu.CompilerParams(vmem_limit_bytes=16 * 1024 * 1024)
CLASS = 8
HALF = CLASS // 2


def split(x):
    high = x.astype(BF16)
    return high, (x - high.astype(F32)).astype(BF16)


def pack_weight_grad(piece):
    flat = jnp.concatenate([piece[:, :E], piece[:, E:]], axis=0)
    high, low = split(flat)
    return jnp.concatenate([high, low], axis=0)


def unpack_weight_grad(packed):
    wide = packed.astype(F32)
    return wide[:16] + wide[16:]


def preload_kernel(tiles, held, sems):
    copies = [pltpu.make_async_copy(tiles.at[c], held.at[c], sems.at[c]) for c in range(CHUNKS)]
    for copy in copies:
        copy.start()
    for copy in copies:
        copy.wait()


def sweep(count, product, add):
    def chunk_step(c, carry):
        left = count - c * GROUP

        @pl.when(left >= GROUP)
        def _():
            for u0 in range(0, GROUP, 4):
                values = [product(c, u, c * GROUP + u) for u in range(u0, u0 + 4)]
                for k, value in enumerate(values):
                    add(c * GROUP + u0 + k, value)

        @pl.when(left < GROUP)
        def _():
            def one(u, inner):
                add(c * GROUP + u, product(c, u, c * GROUP + u))
                return inner

            lax.fori_loop(0, left, one, 0)

        return carry

    lax.fori_loop(0, (count + GROUP - 1) // GROUP, chunk_step, 0)


def chip_first(row, core):
    return jnp.bitwise_xor(jnp.bitwise_and(row, 1), core) * NCHIP + lax.shift_right_logical(row, 1)


def forward_kernel(count, rows, places, core, tiles, mine, peer, near, far, source, total, sems):
    arrivals = [
        pltpu.make_async_copy(mine, source.at[pl.ds(0, NZ)], sems.at[0]),
        pltpu.make_async_copy(peer, source.at[pl.ds(NZ, NZ)], sems.at[1]),
    ]
    for copy in arrivals:
        copy.start()
    total[...] = jnp.zeros_like(total)
    for copy in arrivals:
        copy.wait()

    def product(c, u, t):
        return jnp.dot(tiles[c, u], source[places[t]], preferred_element_type=F32)

    def add(t, value):
        total[chip_first(rows[t], core[0])] += value

    sweep(count[0], product, add)
    near[...] = total[:NCHIP].astype(BF16)
    far[...] = total[NCHIP:].astype(BF16)


def chip_kernel(near, far, both):
    both[...] = (near[...].astype(F32) + far[...].astype(F32)).astype(BF16)


def node_kernel(terms, scale, bias, weight, grad_out, output, pack):
    gathered = terms[0].astype(F32)
    for k in range(1, NCHIP):
        gathered = gathered + terms[k].astype(F32)
    high, low = split(gathered)
    w = weight[...]
    summed = jnp.dot(high, w, preferred_element_type=F32) + jnp.dot(low, w, preferred_element_type=F32)
    square = jnp.broadcast_to(scale[...], (E, E)).T
    r = jnp.concatenate([square, square], axis=1)
    hidden = r * summed + bias[...]
    s = jax.nn.sigmoid(hidden)
    output[...] = (hidden * s).astype(BF16)
    d_hidden = grad_out[...].astype(F32) * s * (1.0 + hidden * (1.0 - s))
    scaled = (r * d_hidden).astype(BF16)
    back = lax.dot_general(w, scaled, (((1,), (1,)), ((), ())), preferred_element_type=F32).astype(BF16)
    first = (((0,), (0,)), ((), ()))
    grad = lax.dot_general(high, scaled, first, preferred_element_type=F32)
    grad = grad + lax.dot_general(low, scaled, first, preferred_element_type=F32)
    for k in range(NCHIP):
        pack[k, pl.ds(0, E)] = back
        for c in range(2):
            first_row = 16 * k + 8 * c
            pack[k, pl.ds(E + GW * c, GW)] = pack_weight_grad(grad[first_row : first_row + 8])


def backward_kernel(count, rows, places, core, tiles, packed, keep, up, down, up2, down2, total):
    total[...] = jnp.zeros_like(total)

    def product(c, u, t):
        block = chip_first(rows[t], 0)
        return jnp.dot(packed[block, pl.ds(0, E)], tiles[c, u], preferred_element_type=F32)

    def add(t, value):
        total[places[t]] += value

    sweep(count[0], product, add)
    own = pl.ds(pl.multiple_of(E + GW * core[0], GW), GW)
    grad = unpack_weight_grad(packed[0, own])
    for k in range(1, NC):
        grad = grad + unpack_weight_grad(packed[k, own])
    high, low = split(grad)
    for ref, first, size, tail in (
        (keep, 0, CLASS, True),
        (up, CLASS, CLASS, True),
        (up2, 2 * CLASS, HALF, True),
        (down2, 2 * CLASS + HALF, HALF, False),
        (down, 3 * CLASS, CLASS, True),
    ):
        for k in range(size):
            ref[pl.ds(k * E, E)] = total[first + k].astype(BF16)
        if tail:
            ref[pl.ds(size * E, 16)] = high
            ref[pl.ds(size * E + 16, 16)] = low


def class_kernel(keep, up, down, up2, down2, pack):
    for k in range(CLASS):
        rows = pl.ds(k * E, E)
        value = keep[rows].astype(F32) + up[rows].astype(F32) + down[rows].astype(F32)
        if k < HALF:
            value = value + up2[rows].astype(F32)
        else:
            value = value + down2[pl.ds((k - HALF) * E, E)].astype(F32)
        pack[k // 2, pl.ds((k % 2) * E, E)] = value.astype(BF16)
    tail = pl.ds(CLASS * E, GW)
    grad = unpack_weight_grad(keep[tail]) + unpack_weight_grad(up[tail])
    grad = grad + unpack_weight_grad(down[tail]) + unpack_weight_grad(up2[pl.ds(HALF * E, GW)])
    high, low = split(grad)
    for h in range(4):
        pack[h, pl.ds(2 * E, 16)] = high
        pack[h, pl.ds(2 * E + 16, 16)] = low


def column_kernel(terms, mine, other, grad_piece):
    value = terms[0].astype(F32)
    for h in range(1, 4):
        value = value + terms[h].astype(F32)
    mine[...] = value[:E]
    other[...] = value[E : 2 * E]
    both = value[2 * E : 2 * E + 16] + value[2 * E + 16 : 2 * E + 32]
    piece = jnp.concatenate([both[:8], both[8:]], axis=1)
    for k in range(NX * NCHIP):
        grad_piece[pl.ds(8 * k, 8)] = piece


def last_kernel(mine, came, pieces, grad_features, grad_weight):
    grad_features[...] = (mine[...] + came[...]).T.astype(BF16)
    for c in range(2):
        for k in range(NCHIP):
            first = 8 * (NX * NCHIP * c + k)
            piece = pieces[pl.ds(first, 8)] + pieces[pl.ds(first + 8 * NCHIP, 8)]
            grad_weight[pl.ds(16 * k + 8 * c, 8)] = piece


def shape(dims, kind=BF16):
    return jax.ShapeDtypeStruct(dims, kind)


def on_device(features, grad_out, row_scale, out_bias, weight, tile_vals, tile_rows, tile_cols, tile_count):
    rows = tile_rows.reshape(SLOTS)
    cols = tile_cols.reshape(SLOTS)
    count = tile_count.reshape(1)
    core = lax.axis_index("core").astype(jnp.int32).reshape(1)
    swap = [(0, 1), (1, 0)]

    def up_z(x, step):
        return lax.ppermute(x, Z, [(k, (k + step) % NZ) for k in range(NZ)])

    flipped = jnp.bitwise_xor(cols // NZ, lax.axis_index("xl"))
    residue = jnp.mod(cols - lax.axis_index("zl"), 4)
    places = (residue * CLASS + (cols // 4) % 4 * 2 + flipped).astype(jnp.int32)
    sources = (flipped * NZ + cols % NZ).astype(jnp.int32)

    near = lax.all_gather(features, Z, axis=0, tiled=True).reshape(NZ, E, E)
    peer = lax.ppermute(near, "xl", swap)
    stored, _ = lax.optimization_barrier((tile_vals.reshape(CHUNKS, GROUP, E, E), near))
    tiles = pl.pallas_call(
        preload_kernel,
        out_shape=pltpu.VMEM((CHUNKS, GROUP, E, E), BF16),
        in_specs=[ANY],
        out_specs=VMEM,
        scratch_shapes=[pltpu.SemaphoreType.DMA((CHUNKS,))],
        compiler_params=PARAMS,
        cost_estimate=pl.CostEstimate(flops=0, bytes_accessed=8 * 1024 * 1024, transcendentals=0),
        name="preload",
    )(stored)
    half = shape((NCHIP, E, E))
    mine, far = pl.pallas_call(
        forward_kernel,
        out_shape=(half, half),
        in_specs=[SMEM] * 4 + [VMEM] + [ANY] * 2,
        out_specs=(VMEM, VMEM),
        scratch_shapes=[
            pltpu.VMEM((NR, E, E), BF16),
            pltpu.VMEM((NC, E, E), F32),
            pltpu.SemaphoreType.DMA((2,)),
        ],
        compiler_params=PARAMS,
        name="forward_sweep",
    )(count, rows, sources, core, tiles, near, peer)
    came = lax.ppermute(far, "core", swap)
    partial = pl.pallas_call(
        chip_kernel,
        out_shape=half,
        in_specs=[VMEM] * 2,
        out_specs=VMEM,
        compiler_params=PARAMS,
        name="chip_sum",
    )(mine, came)
    terms = lax.all_to_all(partial, CHIP, 0, 0, tiled=True)
    output, pack = pl.pallas_call(
        node_kernel,
        out_shape=(shape((E, WIDE)), shape((NCHIP, PACK, E))),
        in_specs=[VMEM] * 5,
        out_specs=(VMEM, VMEM),
        compiler_params=PARAMS,
        name="node_update",
    )(terms, row_scale.reshape(1, E), out_bias.reshape(1, WIDE), weight, grad_out)
    packed = lax.all_to_all(pack, CHIP, 0, 0, tiled=True)
    packed = lax.all_gather(packed, "core", axis=0, tiled=True)

    def line(blocks, tail=GW):
        return shape((blocks * E + tail, E))

    keep, up, down, up2, down2 = pl.pallas_call(
        backward_kernel,
        out_shape=(line(CLASS), line(CLASS), line(CLASS), line(HALF), line(HALF, 0)),
        in_specs=[SMEM] * 4 + [VMEM] * 2,
        out_specs=(VMEM,) * 5,
        scratch_shapes=[pltpu.VMEM((NR, E, E), F32)],
        compiler_params=PARAMS,
        name="backward_sweep",
    )(count, rows, places, core, tiles, packed)
    arrived = [up_z(up, 1), up_z(down, -1), up_z(up2, 2), up_z(down2, -2)]
    classes = pl.pallas_call(
        class_kernel,
        out_shape=shape((4, 2 * E + GW, E)),
        in_specs=[VMEM] * 5,
        out_specs=VMEM,
        compiler_params=PARAMS,
        name="class_sum",
    )(keep, *arrived)
    column = lax.all_to_all(classes, "zh", 0, 0, tiled=True)
    mine, other, piece = pl.pallas_call(
        column_kernel,
        out_shape=(shape((E, E), F32), shape((E, E), F32), shape((NX * NCHIP * 8, WIDE), F32)),
        in_specs=[VMEM],
        out_specs=(VMEM,) * 3,
        compiler_params=PARAMS,
        name="column_sum",
    )(column)
    came = lax.ppermute(other, "xl", swap)
    grads = lax.all_to_all(piece, ("xl",) + CHIP, 0, 0, tiled=True)
    grads = lax.all_gather(grads, "core", axis=0, tiled=True)
    grad_features, grad_weight = pl.pallas_call(
        last_kernel,
        out_shape=(shape((E, E)), shape((E, WIDE), F32)),
        in_specs=[VMEM] * 3,
        out_specs=(VMEM, VMEM),
        compiler_params=PARAMS,
        name="last_sum",
    )(mine, came, grads)
    return output, grad_features, grad_weight


def solution(mesh):
    fine = Mesh(mesh.devices.reshape(SIZES), AXES)
    by_row = ROW + COL
    by_col = COL + ROW
    return jax.shard_map(
        on_device,
        mesh=fine,
        in_specs=(
            P(by_col, None),
            P(by_row, None),
            P(by_row),
            P(),
            P(),
            P(ROW, COL, None, None, None),
            P(ROW, COL, None),
            P(ROW, COL, None),
            P(ROW, COL),
        ),
        out_specs=(P(by_row, None), P(by_col, None), P()),
        check_vma=False,
    )
```

```python
import jax
import jax.numpy as jnp
from jax import lax
from jax.experimental import pallas as pl
from jax.experimental.pallas import tpu as pltpu
from jax.sharding import Mesh
from jax.sharding import PartitionSpec as P

F32 = jnp.float32
BF16 = jnp.bfloat16
Z = ("zh", "zl")
ROW = ("xl",) + Z
CHIP = ("xh", "y")
COL = CHIP + ("core",)
AXES = ROW + COL
SIZES = (2, 4, 4, 2, 4, 2)

E = 128
WIDE = 256
SLOTS = 128
GROUP = 16
CHUNKS = SLOTS // GROUP
NZ, NX, NC = 16, 2, 16
NR = NX * NZ
GW = 32
PACK = E + GW
UNROLL = 64
NCHIP = 8

ANY = pl.BlockSpec(memory_space=pl.ANY)
VMEM = pl.BlockSpec(memory_space=pltpu.VMEM)
SMEM = pl.BlockSpec(memory_space=pltpu.SMEM)
PARAMS = pltpu.CompilerParams(vmem_limit_bytes=16 * 1024 * 1024)
CLASS = 8
HALF = CLASS // 2


def split(x):
    high = x.astype(BF16)
    return high, (x - high.astype(F32)).astype(BF16)


def preload_kernel(tiles, held, sems):
    parts = [pl.ds(c * GROUP, GROUP) for c in range(CHUNKS)]
    copies = [pltpu.make_async_copy(tiles.at[p], held.at[p], sems.at[c]) for c, p in enumerate(parts)]
    for copy in copies:
        copy.start()
    for copy in copies:
        copy.wait()


def sweep(count, left, right, target, total, spare):
    def step(c, carry):
        for u in range(UNROLL):
            t = c * UNROLL + u
            place = jnp.where(t < count, target(t), spare)
            total[place] += jnp.dot(left(t), right(t), preferred_element_type=F32)
        return carry

    lax.fori_loop(0, (count + UNROLL - 1) // UNROLL, step, 0)


def chip_first(row, core):
    return jnp.bitwise_xor(jnp.bitwise_and(row, 1), core) * NCHIP + lax.shift_right_logical(row, 1)


def forward_kernel(count, rows, places, core, tiles, mine, peer, near, far, source, total, sems):
    arrivals = [
        pltpu.make_async_copy(mine, source.at[pl.ds(0, NZ)], sems.at[0]),
        pltpu.make_async_copy(peer, source.at[pl.ds(NZ, NZ)], sems.at[1]),
    ]
    for copy in arrivals:
        copy.start()
    total[...] = jnp.zeros_like(total)
    for copy in arrivals:
        copy.wait()

    sweep(
        count[0],
        lambda t: tiles[t],
        lambda t: source[places[t]],
        lambda t: chip_first(rows[t], core[0]),
        total,
        NC,
    )
    near[...] = total[:NCHIP].astype(BF16)
    far[...] = total[NCHIP:NC].astype(BF16)


def chip_kernel(near, far, both):
    both[...] = (near[...].astype(F32) + far[...].astype(F32)).astype(BF16)


def node_kernel(terms, scale, bias, weight, grad_out, output, pack):
    gathered = terms[0].astype(F32)
    for k in range(1, NCHIP):
        gathered = gathered + terms[k].astype(F32)
    high, low = split(gathered)
    w = weight[...]
    summed = jnp.dot(high, w, preferred_element_type=F32) + jnp.dot(low, w, preferred_element_type=F32)
    square = jnp.broadcast_to(scale[...], (E, E)).T
    r = jnp.concatenate([square, square], axis=1)
    hidden = r * summed + bias[...]
    s = jax.nn.sigmoid(hidden)
    output[...] = (hidden * s).astype(BF16)
    d_hidden = grad_out[...].astype(F32) * s * (1.0 + hidden * (1.0 - s))
    scaled = (r * d_hidden).astype(BF16)
    back = lax.dot_general(w, scaled, (((1,), (1,)), ((), ())), preferred_element_type=F32).astype(BF16)
    first = (((0,), (0,)), ((), ()))
    grad = lax.dot_general(high, scaled, first, preferred_element_type=F32)
    grad = grad + lax.dot_general(low, scaled, first, preferred_element_type=F32)
    for k in range(NCHIP):
        pack[k, pl.ds(0, E)] = back
        share = grad[16 * k : 16 * k + 16]
        pack[k, pl.ds(E, 16)] = share[:, :E].astype(BF16)
        pack[k, pl.ds(E + 16, 16)] = share[:, E:].astype(BF16)


def backward_kernel(count, rows, places, tiles, packed, keep, up, down, up2, down2, total):
    total[...] = jnp.zeros_like(total)

    sweep(
        count[0],
        lambda t: packed[chip_first(rows[t], 0), pl.ds(0, E)],
        lambda t: tiles[t],
        lambda t: places[t],
        total,
        NR,
    )
    grad = packed[0, pl.ds(E, GW)].astype(F32)
    for k in range(1, NC):
        grad = grad + packed[k, pl.ds(E, GW)].astype(F32)
    sent = grad.astype(BF16)
    for ref, first, size, tail in (
        (keep, 0, CLASS, True),
        (up, CLASS, CLASS, True),
        (up2, 2 * CLASS, HALF, True),
        (down2, 2 * CLASS + HALF, HALF, False),
        (down, 3 * CLASS, CLASS, True),
    ):
        for k in range(size):
            ref[pl.ds(k * E, E)] = total[first + k].astype(BF16)
        if tail:
            ref[pl.ds(size * E, GW)] = sent


def class_kernel(keep, up, down, up2, down2, mine, other):
    for k in range(CLASS):
        rows = pl.ds(k * E, E)
        value = keep[rows].astype(F32) + up[rows].astype(F32) + down[rows].astype(F32)
        if k < HALF:
            value = value + up2[rows].astype(F32)
        else:
            value = value + down2[pl.ds((k - HALF) * E, E)].astype(F32)
        target = pl.ds(k // 2 * E, E)
        if k % 2 == 0:
            mine[target] = value
        else:
            other[target] = value.astype(BF16)
    tail = pl.ds(CLASS * E, GW)
    grad = keep[tail].astype(F32) + up[tail].astype(F32) + down[tail].astype(F32)
    grad = grad + up2[pl.ds(HALF * E, GW)].astype(F32)
    mine[pl.ds(HALF * E, GW)] = grad
    other[pl.ds(HALF * E, GW)] = grad.astype(BF16)


def pair_kernel(mine, came, pack):
    tail = pl.ds(HALF * E, GW)
    grad = (mine[tail] + came[tail].astype(F32)).astype(BF16)
    for h in range(4):
        rows = pl.ds(h * E, E)
        pack[h, pl.ds(0, E)] = (mine[rows] + came[rows].astype(F32)).astype(BF16)
        pack[h, pl.ds(E, GW)] = grad


def last_kernel(terms, grad_features, pieces):
    value = terms[0].astype(F32)
    for h in range(1, 4):
        value = value + terms[h].astype(F32)
    grad_features[...] = value[:E].T.astype(BF16)
    share = jnp.concatenate([value[E : E + 16], value[E + 16 :]], axis=1)
    for k in range(NCHIP):
        pieces[k] = share


def shape(dims, kind=BF16):
    return jax.ShapeDtypeStruct(dims, kind)


def on_device(features, grad_out, row_scale, out_bias, weight, tile_vals, tile_rows, tile_cols, tile_count):
    rows = tile_rows.reshape(SLOTS)
    cols = tile_cols.reshape(SLOTS)
    count = tile_count.reshape(1)
    core = lax.axis_index("core").astype(jnp.int32).reshape(1)
    swap = [(0, 1), (1, 0)]

    def up_z(x, step):
        return lax.ppermute(x, Z, [(k, (k + step) % NZ) for k in range(NZ)])

    flipped = jnp.bitwise_xor(cols // NZ, lax.axis_index("xl"))
    residue = jnp.mod(cols - lax.axis_index("zl"), 4)
    places = (residue * CLASS + (cols // 4) % 4 * 2 + flipped).astype(jnp.int32)
    sources = (flipped * NZ + cols % NZ).astype(jnp.int32)

    near = lax.all_gather(features, Z, axis=0, tiled=True).reshape(NZ, E, E)
    peer = lax.ppermute(near, "xl", swap)
    stored, _ = lax.optimization_barrier((tile_vals.reshape(SLOTS, E, E), near))
    tiles = pl.pallas_call(
        preload_kernel,
        out_shape=pltpu.VMEM((SLOTS, E, E), BF16),
        in_specs=[ANY],
        out_specs=VMEM,
        scratch_shapes=[pltpu.SemaphoreType.DMA((CHUNKS,))],
        compiler_params=PARAMS,
        cost_estimate=pl.CostEstimate(flops=0, bytes_accessed=8 * 1024 * 1024, transcendentals=0),
        name="preload",
    )(stored)
    half = shape((NCHIP, E, E))
    mine, far = pl.pallas_call(
        forward_kernel,
        out_shape=(half, half),
        in_specs=[SMEM] * 4 + [VMEM] + [ANY] * 2,
        out_specs=(VMEM, VMEM),
        scratch_shapes=[
            pltpu.VMEM((NR, E, E), BF16),
            pltpu.VMEM((NC + 1, E, E), F32),
            pltpu.SemaphoreType.DMA((2,)),
        ],
        compiler_params=PARAMS,
        name="forward_sweep",
    )(count, rows, sources, core, tiles, near, peer)
    came = lax.ppermute(far, "core", swap)
    partial = pl.pallas_call(
        chip_kernel,
        out_shape=half,
        in_specs=[VMEM] * 2,
        out_specs=VMEM,
        compiler_params=PARAMS,
        name="chip_sum",
    )(mine, came)
    terms = lax.all_to_all(partial, CHIP, 0, 0, tiled=True)
    output, pack = pl.pallas_call(
        node_kernel,
        out_shape=(shape((E, WIDE)), shape((NCHIP, PACK, E))),
        in_specs=[VMEM] * 5,
        out_specs=(VMEM, VMEM),
        compiler_params=PARAMS,
        name="node_update",
    )(terms, row_scale.reshape(1, E), out_bias.reshape(1, WIDE), weight, grad_out)
    packed = lax.all_to_all(pack, CHIP, 0, 0, tiled=True)
    packed = lax.all_gather(packed, "core", axis=0, tiled=True)

    def line(blocks, tail=GW):
        return shape((blocks * E + tail, E))

    keep, up, down, up2, down2 = pl.pallas_call(
        backward_kernel,
        out_shape=(line(CLASS), line(CLASS), line(CLASS), line(HALF), line(HALF, 0)),
        in_specs=[SMEM] * 3 + [VMEM] * 2,
        out_specs=(VMEM,) * 5,
        scratch_shapes=[pltpu.VMEM((NR + 1, E, E), F32)],
        compiler_params=PARAMS,
        name="backward_sweep",
    )(count, rows, places, tiles, packed)
    arrived = [up_z(up, 1), up_z(down, -1), up_z(up2, 2), up_z(down2, -2)]
    mine, other = pl.pallas_call(
        class_kernel,
        out_shape=(shape((HALF * E + GW, E), F32), line(HALF)),
        in_specs=[VMEM] * 5,
        out_specs=(VMEM, VMEM),
        compiler_params=PARAMS,
        name="class_sum",
    )(keep, *arrived)
    came = lax.ppermute(other, "xl", swap)
    pairs = pl.pallas_call(
        pair_kernel,
        out_shape=shape((4, E + GW, E)),
        in_specs=[VMEM] * 2,
        out_specs=VMEM,
        compiler_params=PARAMS,
        name="pair_sum",
    )(mine, came)
    column = lax.all_to_all(pairs, "zh", 0, 0, tiled=True)
    grad_features, pieces = pl.pallas_call(
        last_kernel,
        out_shape=(shape((E, E)), shape((NCHIP, 16, WIDE), F32)),
        in_specs=[VMEM],
        out_specs=(VMEM, VMEM),
        compiler_params=PARAMS,
        name="last_sum",
    )(column)
    grad_weight = lax.all_to_all(pieces, CHIP, 0, 0, tiled=True).reshape(E, WIDE)
    return output, grad_features, grad_weight


def solution(mesh):
    fine = Mesh(mesh.devices.reshape(SIZES), AXES)
    by_row = ROW + COL
    by_col = COL + ROW
    return jax.shard_map(
        on_device,
        mesh=fine,
        in_specs=(
            P(by_col, None),
            P(by_row, None),
            P(by_row),
            P(),
            P(),
            P(ROW, COL, None, None, None),
            P(ROW, COL, None),
            P(ROW, COL, None),
            P(ROW, COL),
        ),
        out_specs=(P(by_row, None), P(by_col, None), P()),
        check_vma=False,
    )
```

```python
import jax
import jax.numpy as jnp
from jax import lax
from jax.experimental import pallas as pl
from jax.experimental.pallas import tpu as pltpu
from jax.sharding import Mesh
from jax.sharding import PartitionSpec as P

F32 = jnp.float32
BF16 = jnp.bfloat16
Z = ("zh", "zl")
ROW = ("xl",) + Z
CHIP = ("xh", "y")
COL = CHIP + ("core",)
FAR = ("xl", "zh")
AXES = ROW + COL
SIZES = (2, 4, 4, 2, 4, 2)

E = 128
WIDE = 256
SLOTS = 128
GROUP = 16
CHUNKS = SLOTS // GROUP
NZ, NX, NC = 16, 2, 16
NR = NX * NZ
GW = 32
PACK = E + GW
UNROLL = 64
NCHIP = 8

ANY = pl.BlockSpec(memory_space=pl.ANY)
VMEM = pl.BlockSpec(memory_space=pltpu.VMEM)
SMEM = pl.BlockSpec(memory_space=pltpu.SMEM)
PARAMS = pltpu.CompilerParams(vmem_limit_bytes=16 * 1024 * 1024)
CLASS = 8


def split(x):
    high = x.astype(BF16)
    return high, (x - high.astype(F32)).astype(BF16)


def preload_kernel(tiles, held, sems):
    parts = [pl.ds(c * GROUP, GROUP) for c in range(CHUNKS)]
    copies = [pltpu.make_async_copy(tiles.at[p], held.at[p], sems.at[c]) for c, p in enumerate(parts)]
    for copy in copies:
        copy.start()
    for copy in copies:
        copy.wait()


def sweep(count, left, right, target, total, spare):
    def step(c, carry):
        for u in range(UNROLL):
            t = c * UNROLL + u
            place = jnp.where(t < count, target(t), spare)
            total[place] += jnp.dot(left(t), right(t), preferred_element_type=F32)
        return carry

    lax.fori_loop(0, (count + UNROLL - 1) // UNROLL, step, 0)


def chip_first(row, core):
    return jnp.bitwise_xor(jnp.bitwise_and(row, 1), core) * NCHIP + lax.shift_right_logical(row, 1)


def forward_kernel(count, rows, places, core, tiles, mine, peer, near, far, source, total, sems):
    arrivals = [
        pltpu.make_async_copy(mine, source.at[pl.ds(0, NZ)], sems.at[0]),
        pltpu.make_async_copy(peer, source.at[pl.ds(NZ, NZ)], sems.at[1]),
    ]
    for copy in arrivals:
        copy.start()
    total[...] = jnp.zeros_like(total)
    for copy in arrivals:
        copy.wait()

    sweep(
        count[0],
        lambda t: tiles[t],
        lambda t: source[places[t]],
        lambda t: chip_first(rows[t], core[0]),
        total,
        NC,
    )
    near[...] = total[:NCHIP].astype(BF16)
    far[...] = total[NCHIP:NC].astype(BF16)


def chip_kernel(near, far, both):
    both[...] = (near[...].astype(F32) + far[...].astype(F32)).astype(BF16)


def node_kernel(terms, scale, bias, weight, grad_out, output, pack):
    gathered = terms[0].astype(F32)
    for k in range(1, NCHIP):
        gathered = gathered + terms[k].astype(F32)
    high, low = split(gathered)
    w = weight[...]
    summed = jnp.dot(high, w, preferred_element_type=F32) + jnp.dot(low, w, preferred_element_type=F32)
    square = jnp.broadcast_to(scale[...], (E, E)).T
    r = jnp.concatenate([square, square], axis=1)
    hidden = r * summed + bias[...]
    s = jax.nn.sigmoid(hidden)
    output[...] = (hidden * s).astype(BF16)
    d_hidden = grad_out[...].astype(F32) * s * (1.0 + hidden * (1.0 - s))
    scaled = (r * d_hidden).astype(BF16)
    back = lax.dot_general(w, scaled, (((1,), (1,)), ((), ())), preferred_element_type=F32).astype(BF16)
    first = (((0,), (0,)), ((), ()))
    grad = lax.dot_general(high, scaled, first, preferred_element_type=F32)
    grad = grad + lax.dot_general(low, scaled, first, preferred_element_type=F32)
    for k in range(NCHIP):
        pack[k, pl.ds(0, E)] = back
        share = grad[16 * k : 16 * k + 16]
        pack[k, pl.ds(E, 16)] = share[:, :E].astype(BF16)
        pack[k, pl.ds(E + 16, 16)] = share[:, E:].astype(BF16)


def backward_kernel(count, rows, places, tiles, packed, keep, up, down, across, total):
    total[...] = jnp.zeros_like(total)

    sweep(
        count[0],
        lambda t: packed[chip_first(rows[t], 0), pl.ds(0, E)],
        lambda t: tiles[t],
        lambda t: places[t],
        total,
        NR,
    )
    grad = packed[0, pl.ds(E, GW)].astype(F32)
    for k in range(1, NC):
        grad = grad + packed[k, pl.ds(E, GW)].astype(F32)
    sent = grad.astype(BF16)
    for b, ref in enumerate((keep, up, across, down)):
        for k in range(CLASS):
            ref[pl.ds(k * E, E)] = total[b * CLASS + k].astype(BF16)
        ref[pl.ds(CLASS * E, GW)] = sent


def class_kernel(keep, up, down, across, pack):
    def value(rows):
        near = keep[rows].astype(F32) + across[rows].astype(F32)
        return (near + (up[rows].astype(F32) + down[rows].astype(F32))).astype(BF16)

    share = value(pl.ds(CLASS * E, GW))
    for k in range(CLASS):
        pack[k, pl.ds(0, E)] = value(pl.ds(k * E, E))
        pack[k, pl.ds(E, GW)] = share


def last_kernel(terms, grad_features, pieces):
    value = terms[0].astype(F32)
    for k in range(1, CLASS):
        value = value + terms[k].astype(F32)
    grad_features[...] = value[:E].T.astype(BF16)
    share = jnp.concatenate([value[E : E + 16], value[E + 16 :]], axis=1)
    for k in range(NCHIP):
        pieces[k] = share


def shape(dims, kind=BF16):
    return jax.ShapeDtypeStruct(dims, kind)


def on_device(features, grad_out, row_scale, out_bias, weight, tile_vals, tile_rows, tile_cols, tile_count):
    rows = tile_rows.reshape(SLOTS)
    cols = tile_cols.reshape(SLOTS)
    count = tile_count.reshape(1)
    core = lax.axis_index("core").astype(jnp.int32).reshape(1)
    swap = [(0, 1), (1, 0)]

    def move_z(x, step):
        return lax.ppermute(x, Z, [(k, (k + step(k)) % NZ) for k in range(NZ)])

    def move_across(x):
        return move_z(x, lambda k: 2 if k % 2 == 0 else -2)

    flipped = jnp.bitwise_xor(cols // NZ, lax.axis_index("xl"))
    residue = jnp.mod(cols - lax.axis_index("zl"), 4)
    places = (residue * CLASS + cols // NZ * 4 + cols // 4 % 4).astype(jnp.int32)
    sources = (flipped * NZ + cols % NZ).astype(jnp.int32)

    near = lax.all_gather(features, Z, axis=0, tiled=True).reshape(NZ, E, E)
    peer = lax.ppermute(near, "xl", swap)
    stored, _ = lax.optimization_barrier((tile_vals.reshape(SLOTS, E, E), near))
    tiles = pl.pallas_call(
        preload_kernel,
        out_shape=pltpu.VMEM((SLOTS, E, E), BF16),
        in_specs=[ANY],
        out_specs=VMEM,
        scratch_shapes=[pltpu.SemaphoreType.DMA((CHUNKS,))],
        compiler_params=PARAMS,
        cost_estimate=pl.CostEstimate(flops=0, bytes_accessed=8 * 1024 * 1024, transcendentals=0),
        name="preload",
    )(stored)
    half = shape((NCHIP, E, E))
    mine, far = pl.pallas_call(
        forward_kernel,
        out_shape=(half, half),
        in_specs=[SMEM] * 4 + [VMEM] + [ANY] * 2,
        out_specs=(VMEM, VMEM),
        scratch_shapes=[
            pltpu.VMEM((NR, E, E), BF16),
            pltpu.VMEM((NC + 1, E, E), F32),
            pltpu.SemaphoreType.DMA((2,)),
        ],
        compiler_params=PARAMS,
        name="forward_sweep",
    )(count, rows, sources, core, tiles, near, peer)
    came = lax.ppermute(far, "core", swap)
    partial = pl.pallas_call(
        chip_kernel,
        out_shape=half,
        in_specs=[VMEM] * 2,
        out_specs=VMEM,
        compiler_params=PARAMS,
        name="chip_sum",
    )(mine, came)
    terms = lax.all_to_all(partial, CHIP, 0, 0, tiled=True)
    output, pack = pl.pallas_call(
        node_kernel,
        out_shape=(shape((E, WIDE)), shape((NCHIP, PACK, E))),
        in_specs=[VMEM] * 5,
        out_specs=(VMEM, VMEM),
        compiler_params=PARAMS,
        name="node_update",
    )(terms, row_scale.reshape(1, E), out_bias.reshape(1, WIDE), weight, grad_out)
    packed = lax.all_to_all(pack, CHIP, 0, 0, tiled=True)
    packed = lax.all_gather(packed, "core", axis=0, tiled=True)

    line = shape((CLASS * E + GW, E))
    keep, up, down, across = pl.pallas_call(
        backward_kernel,
        out_shape=(line,) * 4,
        in_specs=[SMEM] * 3 + [VMEM] * 2,
        out_specs=(VMEM,) * 4,
        scratch_shapes=[pltpu.VMEM((NR + 1, E, E), F32)],
        compiler_params=PARAMS,
        name="backward_sweep",
    )(count, rows, places, tiles, packed)
    arrived = [move_z(up, lambda k: 1), move_z(down, lambda k: -1), move_across(across)]
    classes = pl.pallas_call(
        class_kernel,
        out_shape=shape((CLASS, PACK, E)),
        in_specs=[VMEM] * 4,
        out_specs=VMEM,
        compiler_params=PARAMS,
        name="class_sum",
    )(keep, *arrived)
    column = lax.all_to_all(classes, FAR, 0, 0, tiled=True)
    grad_features, pieces = pl.pallas_call(
        last_kernel,
        out_shape=(shape((E, E)), shape((NCHIP, 16, WIDE), F32)),
        in_specs=[VMEM],
        out_specs=(VMEM, VMEM),
        compiler_params=PARAMS,
        name="last_sum",
    )(column)
    grad_weight = lax.all_to_all(pieces, CHIP, 0, 0, tiled=True).reshape(E, WIDE)
    return output, grad_features, grad_weight


def solution(mesh):
    fine = Mesh(mesh.devices.reshape(SIZES), AXES)
    by_row = ROW + COL
    by_col = COL + ROW
    return jax.shard_map(
        on_device,
        mesh=fine,
        in_specs=(
            P(by_col, None),
            P(by_row, None),
            P(by_row),
            P(),
            P(),
            P(ROW, COL, None, None, None),
            P(ROW, COL, None),
            P(ROW, COL, None),
            P(ROW, COL),
        ),
        out_specs=(P(by_row, None), P(by_col, None), P()),
        check_vma=False,
    )
```

```python
import jax
import jax.numpy as jnp
from jax import lax
from jax.experimental import pallas as pl
from jax.experimental.pallas import tpu as pltpu
from jax.sharding import Mesh
from jax.sharding import PartitionSpec as P

F32 = jnp.float32
BF16 = jnp.bfloat16
Z = ("zh", "z1", "z0")
ROW = ("xl",) + Z
CHIP = ("xh", "y")
COL = CHIP + ("core",)
QUAD = ("xl", "z0")
FAR = ("zh", "z1")
AXES = ROW + COL
SIZES = (2, 4, 2, 2, 2, 4, 2)

E = 128
WIDE = 256
SLOTS = 128
GROUP = 16
CHUNKS = SLOTS // GROUP
NZ, NX, NC = 16, 2, 16
NR = NX * NZ
GW = 32
PACK = E + GW
CLASS = 8
LINE = CLASS * E + GW
UNROLL = 64
NCHIP = 8

ANY = pl.BlockSpec(memory_space=pl.ANY)
VMEM = pl.BlockSpec(memory_space=pltpu.VMEM)
SMEM = pl.BlockSpec(memory_space=pltpu.SMEM)
PARAMS = pltpu.CompilerParams(vmem_limit_bytes=16 * 1024 * 1024)


def split(x):
    high = x.astype(BF16)
    return high, (x - high.astype(F32)).astype(BF16)


def preload_kernel(tiles, held, sems):
    parts = [pl.ds(c * GROUP, GROUP) for c in range(CHUNKS)]
    copies = [pltpu.make_async_copy(tiles.at[p], held.at[p], sems.at[c]) for c, p in enumerate(parts)]
    for copy in copies:
        copy.start()
    for copy in copies:
        copy.wait()


def sweep(count, left, right, target, total, spare):
    def step(c, carry):
        for u in range(UNROLL):
            t = c * UNROLL + u
            place = jnp.where(t < count, target(t), spare)
            total[place] += jnp.dot(left(t), right(t), preferred_element_type=F32)
        return carry

    lax.fori_loop(0, (count + UNROLL - 1) // UNROLL, step, 0)


def chip_first(row, core):
    return jnp.bitwise_xor(jnp.bitwise_and(row, 1), core) * NCHIP + lax.shift_right_logical(row, 1)


def forward_kernel(count, rows, places, core, tiles, mine, peer, near, far, source, total, sems):
    arrivals = [
        pltpu.make_async_copy(mine, source.at[pl.ds(0, NZ)], sems.at[0]),
        pltpu.make_async_copy(peer, source.at[pl.ds(NZ, NZ)], sems.at[1]),
    ]
    for copy in arrivals:
        copy.start()
    total[...] = jnp.zeros_like(total)
    for copy in arrivals:
        copy.wait()

    sweep(
        count[0],
        lambda t: tiles[t],
        lambda t: source[places[t]],
        lambda t: chip_first(rows[t], core[0]),
        total,
        NC,
    )
    near[...] = total[:NCHIP].astype(BF16)
    far[...] = total[NCHIP:NC].astype(BF16)


def chip_kernel(near, far, both):
    both[...] = (near[...].astype(F32) + far[...].astype(F32)).astype(BF16)


def node_kernel(terms, scale, bias, weight, grad_out, output, pack):
    gathered = terms[0].astype(F32)
    for k in range(1, NCHIP):
        gathered = gathered + terms[k].astype(F32)
    high, low = split(gathered)
    w = weight[...]
    summed = jnp.dot(high, w, preferred_element_type=F32) + jnp.dot(low, w, preferred_element_type=F32)
    square = jnp.broadcast_to(scale[...], (E, E)).T
    r = jnp.concatenate([square, square], axis=1)
    hidden = r * summed + bias[...]
    s = jax.nn.sigmoid(hidden)
    output[...] = (hidden * s).astype(BF16)
    d_hidden = grad_out[...].astype(F32) * s * (1.0 + hidden * (1.0 - s))
    scaled = (r * d_hidden).astype(BF16)
    back = lax.dot_general(w, scaled, (((1,), (1,)), ((), ())), preferred_element_type=F32).astype(BF16)
    first = (((0,), (0,)), ((), ()))
    grad = lax.dot_general(high, scaled, first, preferred_element_type=F32)
    grad = grad + lax.dot_general(low, scaled, first, preferred_element_type=F32)
    for k in range(NCHIP):
        pack[k, pl.ds(0, E)] = back
        share = grad[16 * k : 16 * k + 16]
        pack[k, pl.ds(E, 16)] = share[:, :E].astype(BF16)
        pack[k, pl.ds(E + 16, 16)] = share[:, E:].astype(BF16)


def backward_kernel(count, rows, places, tiles, packed, parts, total):
    total[...] = jnp.zeros_like(total)

    sweep(
        count[0],
        lambda t: packed[chip_first(rows[t], 0), pl.ds(0, E)],
        lambda t: tiles[t],
        lambda t: places[t],
        total,
        NR,
    )
    grad = packed[0, pl.ds(E, GW)].astype(F32)
    for k in range(1, NC):
        grad = grad + packed[k, pl.ds(E, GW)].astype(F32)
    sent = grad.astype(BF16)
    for b in range(4):
        for k in range(CLASS):
            parts[b, pl.ds(k * E, E)] = total[b * CLASS + k].astype(BF16)
        parts[b, pl.ds(CLASS * E, GW)] = sent


def class_kernel(parts, pack):
    def value(rows):
        first = parts[0, rows].astype(F32) + parts[1, rows].astype(F32)
        return (first + (parts[2, rows].astype(F32) + parts[3, rows].astype(F32))).astype(BF16)

    share = value(pl.ds(CLASS * E, GW))
    for k in range(CLASS):
        pack[k, pl.ds(0, E)] = value(pl.ds(k * E, E))
        pack[k, pl.ds(E, GW)] = share


def last_kernel(terms, grad_features, pieces):
    value = terms[0].astype(F32)
    for k in range(1, CLASS):
        value = value + terms[k].astype(F32)
    grad_features[...] = value[:E].T.astype(BF16)
    share = jnp.concatenate([value[E : E + 16], value[E + 16 :]], axis=1)
    for k in range(NCHIP):
        pieces[k] = share


def shape(dims, kind=BF16):
    return jax.ShapeDtypeStruct(dims, kind)


def on_device(features, grad_out, row_scale, out_bias, weight, tile_vals, tile_rows, tile_cols, tile_count):
    rows = tile_rows.reshape(SLOTS)
    cols = tile_cols.reshape(SLOTS)
    count = tile_count.reshape(1)
    core = lax.axis_index("core").astype(jnp.int32).reshape(1)
    swap = [(0, 1), (1, 0)]

    flipped = jnp.bitwise_xor(cols // NZ, lax.axis_index("xl"))
    places = ((cols // NZ * 2 + cols % 2) * CLASS + cols // 2 % CLASS).astype(jnp.int32)
    sources = (flipped * NZ + cols % NZ).astype(jnp.int32)

    near = lax.all_gather(features, Z, axis=0, tiled=True).reshape(NZ, E, E)
    peer = lax.ppermute(near, "xl", swap)
    stored, _ = lax.optimization_barrier((tile_vals.reshape(SLOTS, E, E), near))
    tiles = pl.pallas_call(
        preload_kernel,
        out_shape=pltpu.VMEM((SLOTS, E, E), BF16),
        in_specs=[ANY],
        out_specs=VMEM,
        scratch_shapes=[pltpu.SemaphoreType.DMA((CHUNKS,))],
        compiler_params=PARAMS,
        cost_estimate=pl.CostEstimate(flops=0, bytes_accessed=8 * 1024 * 1024, transcendentals=0),
        name="preload",
    )(stored)
    half = shape((NCHIP, E, E))
    mine, far = pl.pallas_call(
        forward_kernel,
        out_shape=(half, half),
        in_specs=[SMEM] * 4 + [VMEM] + [ANY] * 2,
        out_specs=(VMEM, VMEM),
        scratch_shapes=[
            pltpu.VMEM((NR, E, E), BF16),
            pltpu.VMEM((NC + 1, E, E), F32),
            pltpu.SemaphoreType.DMA((2,)),
        ],
        compiler_params=PARAMS,
        name="forward_sweep",
    )(count, rows, sources, core, tiles, near, peer)
    came = lax.ppermute(far, "core", swap)
    partial = pl.pallas_call(
        chip_kernel,
        out_shape=half,
        in_specs=[VMEM] * 2,
        out_specs=VMEM,
        compiler_params=PARAMS,
        name="chip_sum",
    )(mine, came)
    terms = lax.all_to_all(partial, CHIP, 0, 0, tiled=True)
    output, pack = pl.pallas_call(
        node_kernel,
        out_shape=(shape((E, WIDE)), shape((NCHIP, PACK, E))),
        in_specs=[VMEM] * 5,
        out_specs=(VMEM, VMEM),
        compiler_params=PARAMS,
        name="node_update",
    )(terms, row_scale.reshape(1, E), out_bias.reshape(1, WIDE), weight, grad_out)
    packed = lax.all_to_all(pack, CHIP, 0, 0, tiled=True)
    packed = lax.all_gather(packed, "core", axis=0, tiled=True)

    parts = pl.pallas_call(
        backward_kernel,
        out_shape=shape((4, LINE, E)),
        in_specs=[SMEM] * 3 + [VMEM] * 2,
        out_specs=VMEM,
        scratch_shapes=[pltpu.VMEM((NR + 1, E, E), F32)],
        compiler_params=PARAMS,
        name="backward_sweep",
    )(count, rows, places, tiles, packed)
    parts = lax.all_to_all(parts, QUAD, 0, 0, tiled=True)
    classes = pl.pallas_call(
        class_kernel,
        out_shape=shape((CLASS, PACK, E)),
        in_specs=[VMEM],
        out_specs=VMEM,
        compiler_params=PARAMS,
        name="class_sum",
    )(parts)
    column = lax.all_to_all(classes, FAR, 0, 0, tiled=True)
    grad_features, pieces = pl.pallas_call(
        last_kernel,
        out_shape=(shape((E, E)), shape((NCHIP, 16, WIDE), F32)),
        in_specs=[VMEM],
        out_specs=(VMEM, VMEM),
        compiler_params=PARAMS,
        name="last_sum",
    )(column)
    grad_weight = lax.all_to_all(pieces, CHIP, 0, 0, tiled=True).reshape(E, WIDE)
    return output, grad_features, grad_weight


def solution(mesh):
    fine = Mesh(mesh.devices.reshape(SIZES), AXES)
    by_row = ROW + COL
    by_col = COL + ROW
    return jax.shard_map(
        on_device,
        mesh=fine,
        in_specs=(
            P(by_col, None),
            P(by_row, None),
            P(by_row),
            P(),
            P(),
            P(ROW, COL, None, None, None),
            P(ROW, COL, None),
            P(ROW, COL, None),
            P(ROW, COL),
        ),
        out_specs=(P(by_row, None), P(by_col, None), P()),
        check_vma=False,
    )
```

```python
import jax
import jax.numpy as jnp
from jax import lax
from jax.experimental import pallas as pl
from jax.experimental.pallas import tpu as pltpu
from jax.sharding import Mesh
from jax.sharding import PartitionSpec as P

F32 = jnp.float32
BF16 = jnp.bfloat16
Z = ("zh", "z1", "z0")
ROW = ("xl",) + Z
CHIP = ("xh", "y")
COL = CHIP + ("core",)
QUAD = ("xl", "z0")
FAR = ("zh", "z1")
AXES = ROW + COL
SIZES = (2, 4, 2, 2, 2, 4, 2)

E = 128
WIDE = 256
SLOTS = 128
GROUP = 16
CHUNKS = SLOTS // GROUP
NZ, NX, NC = 16, 2, 16
NR = NX * NZ
GW = 32
PACK = E + GW
CLASS = 8
GH = GW // 2
LINE = CLASS * E + GH
UNROLL = 64
NCHIP = 8

ANY = pl.BlockSpec(memory_space=pl.ANY)
VMEM = pl.BlockSpec(memory_space=pltpu.VMEM)
SMEM = pl.BlockSpec(memory_space=pltpu.SMEM)
PARAMS = pltpu.CompilerParams(vmem_limit_bytes=16 * 1024 * 1024)


def split(x):
    high = x.astype(BF16)
    return high, (x - high.astype(F32)).astype(BF16)


def preload_kernel(tiles, held, sems):
    parts = [pl.ds(c * GROUP, GROUP) for c in range(CHUNKS)]
    copies = [pltpu.make_async_copy(tiles.at[p], held.at[p], sems.at[c]) for c, p in enumerate(parts)]
    for copy in copies:
        copy.start()
    for copy in copies:
        copy.wait()


def sweep(count, left, right, target, total, spare):
    def step(c, carry):
        for u in range(UNROLL):
            t = c * UNROLL + u
            place = jnp.where(t < count, target(t), spare)
            total[place] += jnp.dot(left(t), right(t), preferred_element_type=F32)
        return carry

    lax.fori_loop(0, (count + UNROLL - 1) // UNROLL, step, 0)


def chip_first(row, core):
    return jnp.bitwise_xor(jnp.bitwise_and(row, 1), core) * NCHIP + lax.shift_right_logical(row, 1)


def forward_kernel(count, rows, places, core, tiles, mine, peer, near, far, source, total, sems):
    arrivals = [
        pltpu.make_async_copy(mine, source.at[pl.ds(0, NZ)], sems.at[0]),
        pltpu.make_async_copy(peer, source.at[pl.ds(NZ, NZ)], sems.at[1]),
    ]
    for copy in arrivals:
        copy.start()
    total[...] = jnp.zeros_like(total)
    for copy in arrivals:
        copy.wait()

    sweep(
        count[0],
        lambda t: tiles[t],
        lambda t: source[places[t]],
        lambda t: chip_first(rows[t], core[0]),
        total,
        NC,
    )
    near[...] = total[:NCHIP].astype(BF16)
    far[...] = total[NCHIP:NC].astype(BF16)


def chip_kernel(near, far, both):
    both[...] = (near[...].astype(F32) + far[...].astype(F32)).astype(BF16)


def node_kernel(terms, scale, bias, weight, grad_out, output, pack):
    gathered = terms[0].astype(F32)
    for k in range(1, NCHIP):
        gathered = gathered + terms[k].astype(F32)
    high, low = split(gathered)
    w = weight[...]
    summed = jnp.dot(high, w, preferred_element_type=F32) + jnp.dot(low, w, preferred_element_type=F32)
    square = jnp.broadcast_to(scale[...], (E, E)).T
    r = jnp.concatenate([square, square], axis=1)
    hidden = r * summed + bias[...]
    s = jax.nn.sigmoid(hidden)
    output[...] = (hidden * s).astype(BF16)
    d_hidden = grad_out[...].astype(F32) * s * (1.0 + hidden * (1.0 - s))
    scaled = (r * d_hidden).astype(BF16)
    back = lax.dot_general(w, scaled, (((1,), (1,)), ((), ())), preferred_element_type=F32).astype(BF16)
    first = (((0,), (0,)), ((), ()))
    grad = lax.dot_general(high, scaled, first, preferred_element_type=F32)
    grad = grad + lax.dot_general(low, scaled, first, preferred_element_type=F32)
    for k in range(NCHIP):
        pack[k, pl.ds(0, E)] = back
        share = grad[16 * k : 16 * k + 16]
        pack[k, pl.ds(E, 16)] = share[:, :E].astype(BF16)
        pack[k, pl.ds(E + 16, 16)] = share[:, E:].astype(BF16)


def backward_kernel(count, rows, places, tiles, packed, parts, total):
    total[...] = jnp.zeros_like(total)

    sweep(
        count[0],
        lambda t: packed[chip_first(rows[t], 0), pl.ds(0, E)],
        lambda t: tiles[t],
        lambda t: places[t],
        total,
        NR,
    )
    grad = packed[0, pl.ds(E, GW)].astype(F32)
    for k in range(1, NC):
        grad = grad + packed[k, pl.ds(E, GW)].astype(F32)
    halves = [jnp.concatenate([grad[8 * x : 8 * x + 8], grad[16 + 8 * x : 24 + 8 * x]], axis=0) for x in range(NX)]
    for b in range(4):
        for k in range(CLASS):
            parts[b, pl.ds(k * E, E)] = total[b * CLASS + k].astype(BF16)
        parts[b, pl.ds(CLASS * E, GH)] = halves[b // 2].astype(BF16)


def class_kernel(parts, pack):
    def value(rows):
        first = parts[0, rows].astype(F32) + parts[1, rows].astype(F32)
        return (first + (parts[2, rows].astype(F32) + parts[3, rows].astype(F32))).astype(BF16)

    share = value(pl.ds(CLASS * E, GH))
    for k in range(CLASS):
        pack[k, pl.ds(0, E)] = value(pl.ds(k * E, E))
        pack[k, pl.ds(E, GH)] = share


def last_kernel(terms, grad_features, pieces):
    value = terms[0].astype(F32)
    for k in range(1, CLASS):
        value = value + terms[k].astype(F32)
    grad_features[...] = value[:E].T.astype(BF16)
    share = jnp.concatenate([value[E : E + 8], value[E + 8 :]], axis=1)
    for k in range(NCHIP * NX):
        pieces[k] = share


def shape(dims, kind=BF16):
    return jax.ShapeDtypeStruct(dims, kind)


def on_device(features, grad_out, row_scale, out_bias, weight, tile_vals, tile_rows, tile_cols, tile_count):
    rows = tile_rows.reshape(SLOTS)
    cols = tile_cols.reshape(SLOTS)
    count = tile_count.reshape(1)
    core = lax.axis_index("core").astype(jnp.int32).reshape(1)
    swap = [(0, 1), (1, 0)]

    flipped = jnp.bitwise_xor(cols // NZ, lax.axis_index("xl"))
    places = ((cols // NZ * 2 + cols % 2) * CLASS + cols // 2 % CLASS).astype(jnp.int32)
    sources = (flipped * NZ + cols % NZ).astype(jnp.int32)

    near = lax.all_gather(features, Z, axis=0, tiled=True).reshape(NZ, E, E)
    peer = lax.ppermute(near, "xl", swap)
    stored, _ = lax.optimization_barrier((tile_vals.reshape(SLOTS, E, E), near))
    tiles = pl.pallas_call(
        preload_kernel,
        out_shape=pltpu.VMEM((SLOTS, E, E), BF16),
        in_specs=[ANY],
        out_specs=VMEM,
        scratch_shapes=[pltpu.SemaphoreType.DMA((CHUNKS,))],
        compiler_params=PARAMS,
        cost_estimate=pl.CostEstimate(flops=0, bytes_accessed=8 * 1024 * 1024, transcendentals=0),
        name="preload",
    )(stored)
    half = shape((NCHIP, E, E))
    mine, far = pl.pallas_call(
        forward_kernel,
        out_shape=(half, half),
        in_specs=[SMEM] * 4 + [VMEM] + [ANY] * 2,
        out_specs=(VMEM, VMEM),
        scratch_shapes=[
            pltpu.VMEM((NR, E, E), BF16),
            pltpu.VMEM((NC + 1, E, E), F32),
            pltpu.SemaphoreType.DMA((2,)),
        ],
        compiler_params=PARAMS,
        name="forward_sweep",
    )(count, rows, sources, core, tiles, near, peer)
    came = lax.ppermute(far, "core", swap)
    partial = pl.pallas_call(
        chip_kernel,
        out_shape=half,
        in_specs=[VMEM] * 2,
        out_specs=VMEM,
        compiler_params=PARAMS,
        name="chip_sum",
    )(mine, came)
    terms = lax.all_to_all(partial, CHIP, 0, 0, tiled=True)
    output, pack = pl.pallas_call(
        node_kernel,
        out_shape=(shape((E, WIDE)), shape((NCHIP, PACK, E))),
        in_specs=[VMEM] * 5,
        out_specs=(VMEM, VMEM),
        compiler_params=PARAMS,
        name="node_update",
    )(terms, row_scale.reshape(1, E), out_bias.reshape(1, WIDE), weight, grad_out)
    packed = lax.all_to_all(pack, CHIP, 0, 0, tiled=True)
    packed = lax.all_gather(packed, "core", axis=0, tiled=True)

    parts = pl.pallas_call(
        backward_kernel,
        out_shape=shape((4, LINE, E)),
        in_specs=[SMEM] * 3 + [VMEM] * 2,
        out_specs=VMEM,
        scratch_shapes=[pltpu.VMEM((NR + 1, E, E), F32)],
        compiler_params=PARAMS,
        name="backward_sweep",
    )(count, rows, places, tiles, packed)
    parts = lax.all_to_all(parts, QUAD, 0, 0, tiled=True)
    classes = pl.pallas_call(
        class_kernel,
        out_shape=shape((CLASS, E + GH, E)),
        in_specs=[VMEM],
        out_specs=VMEM,
        compiler_params=PARAMS,
        name="class_sum",
    )(parts)
    column = lax.all_to_all(classes, FAR, 0, 0, tiled=True)
    grad_features, pieces = pl.pallas_call(
        last_kernel,
        out_shape=(shape((E, E)), shape((NCHIP * NX, 8, WIDE), F32)),
        in_specs=[VMEM],
        out_specs=(VMEM, VMEM),
        compiler_params=PARAMS,
        name="last_sum",
    )(column)
    grad_weight = lax.all_to_all(pieces, CHIP + ("xl",), 0, 0, tiled=True).reshape(E, WIDE)
    return output, grad_features, grad_weight


def solution(mesh):
    fine = Mesh(mesh.devices.reshape(SIZES), AXES)
    by_row = ROW + COL
    by_col = COL + ROW
    return jax.shard_map(
        on_device,
        mesh=fine,
        in_specs=(
            P(by_col, None),
            P(by_row, None),
            P(by_row),
            P(),
            P(),
            P(ROW, COL, None, None, None),
            P(ROW, COL, None),
            P(ROW, COL, None),
            P(ROW, COL),
        ),
        out_specs=(P(by_row, None), P(by_col, None), P()),
        check_vma=False,
    )
```
